256 devices in a mesh: gx: 8 (over y, z_lo), gy: 32 (over z_hi, x, core).
Axes of the slice: x: 4, y: 4, z: 8 (z_hi: 4, z_lo: 2; z = z_hi * 2 + z_lo), core: 2. Of those that a mesh axis runs over, the one named last changes fastest.
Arguments:
- density: float32 [8, 4096, 8192], P(None, 'gx', 'gy'), may hold values from -6 to 6
Outputs:
- refactored: float32 [8, 4096, 8192], P(None, 'gx', 'gy')
The draws below stay inside these ranges and needn't reach their ends.
All inputs are finite; a program needn't handle non-finite values.
Results may differ from the reference program's by a relative error of at most 0.000096.
Values sent between devices are 32-bit elements; how exact they have to be, the bound alone decides.
No kernel may reach another device: no remote copies, remote signals or barrier semaphores. Data moves between devices by JAX's collectives and lax.ppermute only.
A program may use at most 128 MiB of HBM per device.

```python
import math
import jax
import jax.numpy as jnp
from jax import lax

NZ = 8
NX = 4096
NY = 8192


def shard_levels(stream_key, extent, split, least, high):
    level = 1.0
    for axis_at, blocks in split:
        draws = jax.random.uniform(jax.random.fold_in(jax.random.fold_in(stream_key, 6), axis_at), (blocks,), jnp.float32, least / len(split), high / len(split))
        level = level * jnp.repeat(jnp.exp(draws), extent[axis_at] // blocks).reshape((-1,) + (1,) * (len(extent) - 1 - axis_at))
    return level


def noise(rng, shape, scale, bound, cuts=(), kind=jnp.bfloat16):
    values = jax.random.normal(rng, shape, jnp.float32) * scale
    if len(cuts) > 0:
        values = shard_levels(rng, shape, cuts, -0.22, 0.18) * values
    return jnp.clip(values, min=-bound, max=bound).astype(kind)


def setup_inputs(seed: int = 0) -> dict:
    splits = jax.random.split(jax.random.key(seed), 2)
    density = noise(splits[0], (NZ, NX, NY), 1.0, 6.0, ((1, 8), (2, 32)), jnp.float32)
    return dict(density=density)


def split_nodes(field, dimension):
    size_along = field.shape[dimension]
    even_nodes = lax.slice_in_dim(field, 0, size_along, 2, dimension)
    odd_nodes = lax.slice_in_dim(field, 1, size_along, 2, dimension)
    return even_nodes, odd_nodes


def weave_nodes(even_nodes, odd_nodes, dimension):
    stacked = jnp.stack([even_nodes, odd_nodes], dimension + 1)
    grid_shape = list(even_nodes.shape)
    grid_shape[dimension] = grid_shape[dimension] * 2
    return stacked.reshape(grid_shape)


def predict_line(field, dimension):
    even_nodes, odd_nodes = split_nodes(field, dimension)
    following = jnp.roll(even_nodes, -1, dimension)
    return weave_nodes(even_nodes, odd_nodes - 0.5 * (even_nodes + following), dimension)


def mass_apply(field, dimension):
    return (jnp.roll(field, 1, dimension) + 4.0 * field + jnp.roll(field, -1, dimension)) / 6.0


def restrict(field, dimension):
    even_nodes, odd_nodes = split_nodes(field, dimension)
    return even_nodes + 0.5 * (odd_nodes + jnp.roll(odd_nodes, 1, dimension))


def circulant_solve(field, dimension):
    size_along = field.shape[dimension]
    angles = 2.0 * math.pi * jnp.arange(size_along, dtype=jnp.float32) / size_along
    eigen_values = (4.0 + 2.0 * jnp.cos(angles)) / 3.0
    grid_shape = [1] * field.ndim
    grid_shape[dimension] = size_along
    spectrum = jnp.fft.fft(field, axis=dimension) / eigen_values.reshape(grid_shape)
    return jnp.real(jnp.fft.ifft(spectrum, axis=dimension)).astype(field.dtype)


def keep_mask(grid_shape):
    plane_odd = lax.broadcasted_iota(jnp.int32, grid_shape, 0) % 2
    row_odd = lax.broadcasted_iota(jnp.int32, grid_shape, 1) % 2
    column_odd = lax.broadcasted_iota(jnp.int32, grid_shape, 2) % 2
    return ((plane_odd + row_odd + column_odd) > 0).astype(jnp.float32)


def refine_level(field):
    details = predict_line(predict_line(predict_line(field, 1), 2), 0)
    coefficients = details * keep_mask(details.shape).astype(details.dtype)
    loading = coefficients
    for dimension in (1, 2, 0):
        loading = restrict(mass_apply(loading, dimension), dimension)
    correction = circulant_solve(circulant_solve(circulant_solve(loading, 1), 2), 0)
    coarse = field[::2, ::2, ::2] + correction
    return details, coarse


def reference(density):
    details_fine, coarse_fine = refine_level(density)
    details_coarse, coarse_last = refine_level(coarse_fine)
    inner = details_coarse.at[::2, ::2, ::2].set(coarse_last)
    return details_fine.at[::2, ::2, ::2].set(inner)
```

```python
import functools

import jax
import jax.numpy as jnp
import numpy as np
from jax import lax
from jax.experimental import pallas as pl
from jax.experimental.pallas import tpu as pltpu
from jax.sharding import PartitionSpec as P

ROOT = np.sqrt(3.0) - 2.0
CENTRE = 3.0 / np.sqrt(12.0)
F32 = jnp.float32


def line_operators(fine):
    n = fine // 2
    load = np.zeros((3 * n, 3 * fine))
    even = np.zeros((3 * n, 3 * n))
    for j in range(3 * n):
        for at, weight in ((2 * j, 1 / 3), (2 * j - 2, -1 / 6), (2 * j + 2, -1 / 6),
                           (2 * j - 1, 0.5), (2 * j + 1, 0.5)):
            if 0 <= at < 3 * fine:
                load[j, at] = weight
        for at, weight in ((j, 5 / 6), (j - 1, 1 / 12), (j + 1, 1 / 12)):
            if 0 <= at < 3 * n:
                even[j, at] = weight
    place = np.arange(3 * n)
    solve = CENTRE * ROOT ** np.abs(place[:, None] - place[None, :])
    a = (solve @ load)[:, fine:2 * fine]
    d = (solve @ even)[:, n:2 * n]
    near = np.arange(n)
    return dict(
        n=n, a=a[n:2 * n], a_left=a[n - 1], a_right=a[2 * n],
        d=d[n:2 * n], d_left=d[n - 1], d_right=d[2 * n],
        from_left=ROOT ** near, from_right=ROOT ** (n - 1 - near),
    )


def on_even(rows):
    wide = np.zeros(rows.shape[:-1] + (2 * rows.shape[-1],))
    wide[..., ::2] = rows
    return wide


def two_levels(fine):
    one = line_operators(fine)
    two = line_operators(one["n"])
    functionals = dict(
        a_left=two["a_left"], a_right=two["a_right"],
        d_left=on_even(two["d_left"]), d_right=on_even(two["d_right"]),
    )
    return one, two, functionals


def x_tables(fine):
    one, two, f = two_levels(fine)
    n = one["n"]
    rows = n + 8
    own = []
    for kind in ("a", "d"):
        table = np.zeros((rows, one[kind].shape[1]))
        left, right = one[kind + "_left"], one[kind + "_right"]
        table[:n] = one[kind]
        table[n] = right
        table[n + 1] = (f["a_right"] @ one["from_right"]) * left
        table[n + 2] = (f["a_left"] @ one["from_left"]) * right
        table[n + 3] = (f["d_right"] @ one["from_right"]) * left
        table[n + 4] = (f["d_left"] @ one["from_left"]) * right
        own.append(table)
    send = []
    for side in ("left", "right"):
        parts = []
        for kind in ("a", "d", "e"):
            part = np.zeros((16, fine))
            if kind == "e":
                part[8], part[9] = on_even(f["a_" + side]), on_even(f["d_" + side])
            else:
                base, step = (0, 1) if kind == "a" else (4, 2)
                part[base, ::step] = one[kind + "_" + side]
                part[base + 1, ::step] = f["a_" + side] @ one[kind]
                part[base + 2, ::step] = f["d_" + side] @ one[kind]
                part[base + 3, ::step] = one[kind][0]
            parts.append(part)
        send.append(parts)
    receive = np.zeros((rows, 32))
    for base in (0, 4):
        receive[:n, base] = one["from_left"]
        receive[n + 1, base + 1] = 1
        receive[n + 3, base + 2] = 1
        receive[:n, 16 + base] = one["from_right"]
        receive[n + 2, 16 + base + 1] = 1
        receive[n + 4, 16 + base + 2] = 1
        receive[n, 16 + base + 3] = 1
    receive[n + 1, 8] = receive[n + 3, 9] = 1
    receive[n + 2, 16 + 8] = receive[n + 4, 16 + 9] = receive[n, 16 + 10] = 1
    m = n // 2
    level2_a, level2_d = np.zeros((m, rows)), np.zeros((m, rows))
    level2_a[:, :n], level2_d[:, :n] = two["a"], on_even(two["d"])
    level2_a[:, n + 1], level2_a[:, n + 2] = two["from_left"], two["from_right"]
    level2_d[:, n + 3], level2_d[:, n + 4] = two["from_left"], two["from_right"]
    return own, send, receive, np.concatenate([level2_a, level2_d], 0)


def y_tables(fine):
    one, two, f = two_levels(fine)
    n = one["n"]
    kinds = []
    for kind in ("e", "a", "d"):
        table = np.zeros((fine, 2 * n))
        if kind == "e":
            inside = on_even(np.eye(n))
            left = right = np.zeros(fine)
        else:
            widen = on_even if kind == "d" else (lambda rows: rows)
            inside = widen(one[kind])
            left, right = widen(one[kind + "_left"]), widen(one[kind + "_right"])
        table[:, :n] = inside.T
        table[:, n] = right
        table[:, n + 1] = (f["a_right"] @ one["from_right"]) * left
        table[:, n + 2] = (f["a_left"] @ one["from_left"]) * right
        table[:, n + 3] = (f["d_right"] @ one["from_right"]) * left
        table[:, n + 4] = (f["d_left"] @ one["from_left"]) * right
        table[:, n + 8], table[:, n + 9] = left, right
        for at, name in enumerate(("a_left", "a_right", "d_left", "d_right")):
            table[:, n + 10 + at] = f[name] @ inside
        table[:, n + 14] = inside[0]
        kinds.append(-table if kind == "d" else table)
    receive = np.zeros((16, 2 * n))
    receive[1, :n] = one["from_left"]
    receive[3, n + 1] = receive[5, n + 3] = 1
    receive[8, :n] = one["from_right"]
    receive[10, n + 2] = receive[12, n + 4] = receive[14, n] = 1
    m = n // 2
    level2 = np.zeros((3, 2 * n, m))
    level2[0, :n] = on_even(np.eye(m)).T
    level2[1, :n] = two["a"].T
    level2[1, n + 1], level2[1, n + 2] = two["from_left"], two["from_right"]
    level2[2, :n] = -on_even(two["d"]).T
    level2[2, n + 3], level2[2, n + 4] = -two["from_left"], -two["from_right"]
    spread2 = on_even(level2).reshape(6 * n, n)
    return np.concatenate(kinds, 0), receive, spread2, on_even(np.eye(n))


def z_tables(planes):
    n = planes // 2
    predict, spread = np.eye(planes), np.zeros((planes, n))
    mass, restrict, solve = (np.zeros(s) for s in ((planes, planes), (n, planes), (n, n)))
    for i in range(planes):
        for at, weight in ((i, 4 / 6), (i - 1, 1 / 6), (i + 1, 1 / 6)):
            mass[i, at % planes] += weight
        if i % 2:
            predict[i, i - 1] -= 0.5
            predict[i, (i + 1) % planes] -= 0.5
    for j in range(n):
        spread[2 * j, j] = 1
        for at, weight in ((2 * j, 1.0), (2 * j - 1, 0.5), (2 * j + 1, 0.5)):
            restrict[j, at % planes] += weight
        for at, weight in ((j, 4 / 3), (j - 1, 1 / 3), (j + 1, 1 / 3)):
            solve[j, at % n] += weight
    load = np.linalg.inv(solve) @ restrict @ mass
    return (load @ predict).tolist(), (load @ spread).tolist()


def dot(a, b, dims=((1,), (0,))):
    return lax.dot_general(
        a, b, (dims, ((), ())), precision=lax.Precision.HIGHEST, preferred_element_type=F32
    )


def combine(weights, planes):
    total = None
    for weight, plane in zip(weights, planes):
        term = plane * float(weight)
        total = term if total is None else total + term
    return total


def parity_of(axis):
    return (lax.axis_index(axis) % 2).astype(jnp.int32).reshape(1)


def swap(first, second, axis):
    size = lax.axis_size(axis)
    inner = [(i, i ^ 1) for i in range(size)]
    outer = [(i, (i + 1) % size if i % 2 else (i - 1) % size) for i in range(size)]
    return lax.ppermute(first, axis, inner), lax.ppermute(second, axis, outer)


def edge_kernel(z_a, z_d, parity, top, bottom, left_table, right_table, first, second):
    planes = top.shape[0]

    def message(strip, table, row):
        fine = [strip[k] for k in range(planes)]
        even = fine[::2]
        a = [combine(weights, fine) for weights in z_a]
        d = [combine(weights, even) for weights in z_d]
        cat = [jnp.concatenate([a[k], d[k], even[k]], 0) for k in range(planes // 2)]
        out = dot(table[...], jnp.concatenate(cat, 1))
        if row:
            index = lax.broadcasted_iota(jnp.int32, out.shape, 0)
            firsts = jnp.concatenate([strip[k, :1, :] for k in range(0, planes, 2)], 1)
            others = jnp.concatenate([strip[k, :1, :] for k in range(1, planes, 2)], 1)
            out = jnp.where(index == 10, firsts, jnp.where(index == 11, others, out))
        return out

    to_left = message(top, left_table, True)
    to_right = message(bottom, right_table, False)
    odd = parity[0] == 1
    first[...] = jnp.where(odd, to_left, to_right)
    second[...] = jnp.where(odd, to_right, to_left)


def own_kernel(z_a, z_d, low, high, a_table, d_table, y_table, c, column):
    planes, fine, lanes = low.shape
    n, width = fine // 2, 2 * lanes
    halves = (low, high)
    whole = [jnp.concatenate([part[k] for part in halves], 1) for k in range(planes)]
    even = [
        jnp.concatenate([part[k, pl.ds(0, n, stride=2), :] for part in halves], 1)
        for k in range(0, planes, 2)
    ]
    for z in range(planes // 2):
        x_a = dot(a_table[...], combine(z_a[z], whole))
        x_d = dot(d_table[...], combine(z_d[z], even))
        total = dot(x_a, y_table[width:2 * width]) + dot(x_d, y_table[2 * width:])
        c[z] = total
        c[z, :n] = total[:n] + dot(even[z], y_table[:width])
    for k in range(planes):
        column[k:k + 1, :] = low[k].T[:1, :]


def join_kernel(parity, c_own, column, first, second, receive, y_table, c, message):
    half, rows, width = c_own.shape
    odd = parity[0] == 1
    from_left = jnp.where(odd, first[...], second[...])
    from_right = jnp.where(odd, second[...], first[...])
    both = jnp.concatenate([from_left, from_right], 0)
    stacked = jnp.concatenate(
        [both[:, z * width:(z + 1) * width] for z in range(half)], 0
    )
    kind = lax.broadcasted_iota(jnp.int32, stacked.shape, 0) % 16
    typed = jnp.concatenate(
        [
            jnp.where(kind >= 8, stacked, 0.0),
            jnp.where(kind < 4, stacked, 0.0),
            jnp.where((kind >= 4) & (kind < 8), stacked, 0.0),
        ],
        1,
    )
    processed = dot(typed, y_table[...])
    lanes = message.shape[1]
    message[...] = jnp.zeros_like(message)
    for z in range(half):
        field = c_own[z] + dot(receive[...], processed[32 * z:32 * z + 32])
        c[z] = field
        side = field[:, width // 2:].T
        message[:, z * 384:z * 384 + rows] = side[8:16]
    u0 = column[...]
    fine = u0.shape[1]
    plane = lax.broadcasted_iota(jnp.int32, u0.shape, 0)
    lane = lax.broadcasted_iota(jnp.int32, u0.shape, 1)
    after = pltpu.roll(u0, fine - 1, 1)
    for z in range(half):
        for k, row in ((2 * z, 10), (2 * z + 1, 11)):
            corner = from_right[row:row + 1, z * width:z * width + 1]
            after = jnp.where((plane == k) & (lane == fine - 1), corner, after)
    before = pltpu.roll(u0, 1, 1)
    u0 = jnp.where(lane % 2 == 1, u0 - 0.5 * (before + after), u0)
    around = pltpu.roll(u0, 1, 0) + pltpu.roll(u0, 2 * half - 1, 0)
    message[:, lanes - fine:] = jnp.where(plane % 2 == 1, u0 - 0.5 * around, u0)


def detail_kernel(parity, u, first, second, w):
    planes, fine, width = u.shape
    odd = parity[0] == 1
    from_right = jnp.where(odd, second[...], first[...])
    row = lax.broadcasted_iota(jnp.int32, (fine, width), 0)
    lane = lax.broadcasted_iota(jnp.int32, (fine, width), 1)

    def along_x(k):
        plane = u[k]
        at = (k // 2) * width
        halo = from_right[10 + k % 2:11 + k % 2, at:at + width]
        after = jnp.where(row == fine - 1, halo, pltpu.roll(plane, fine - 1, 0))
        before = pltpu.roll(plane, 1, 0)
        return jnp.where(row % 2 == 1, plane - 0.5 * (before + after), plane)

    def along_y(plane):
        after = jnp.where(lane == width - 1, 0.0, pltpu.roll(plane, width - 1, 1))
        before = pltpu.roll(plane, 1, 1)
        return jnp.where(lane % 2 == 1, plane - 0.5 * (before + after), plane)

    start = along_x(0)
    even = start
    for k in range(0, planes, 2):
        w[k] = along_y(even)
        following = start if k + 2 == planes else along_x(k + 2)
        w[k + 1] = along_y(along_x(k + 1) - 0.5 * (even + following))
        even = following


def last_kernel(z_a, z_d, parity, c, w, first, second, receive, x_table, y_table, spread, out, inner):
    half, rows, width = c.shape
    planes, fine, lanes = out.shape
    n, m = fine // 2, width // 2
    at = pl.program_id(0)
    odd = parity[0] == 1
    from_right = jnp.where(odd, second[...], first[...])

    @pl.when(at == 0)
    def _():
        from_left = jnp.where(odd, first[...], second[...])
        both = jnp.concatenate([from_left, from_right], 0)
        coarse = []
        for z in range(half):
            sides = both[:, z * 384:(z + 1) * 384].T[:rows]
            coarse.append(c[z] + dot(sides, receive[...]))

        def along_xy(field):
            after = pltpu.roll(field, rows - 1, 0)
            before = pltpu.roll(field, 1, 0)
            index = lax.broadcasted_iota(jnp.int32, field.shape, 0)
            field = jnp.where(index % 2 == 1, field - 0.5 * (before + after), field)[:n]
            after = pltpu.roll(field, width - 1, 1)
            before = pltpu.roll(field, 1, 1)
            index = lax.broadcasted_iota(jnp.int32, field.shape, 1)
            return jnp.where(index % 2 == 1, field - 0.5 * (before + after), field)[:, :m]

        details = [along_xy(field) for field in coarse]
        for z in range(0, half, 2):
            inner[z] = details[z]
            around = details[z] + details[(z + 2) % half]
            inner[z + 1] = details[z + 1] - 0.5 * around
        level = [dot(x_table[...], field) for field in coarse]
        quarter = n // 2
        level_a = [part[:quarter] for part in level]
        level_d = [part[quarter:] for part in level[::2]]
        mark = lax.broadcasted_iota(jnp.int32, (quarter, m), 1) % 2 == 0
        for z in range(half // 2):
            a = combine(z_a[z], level_a)
            d = combine(z_d[z], level_d)
            here = pl.ds(0, quarter, stride=2)
            values = dot(a, y_table[width:2 * width]) + dot(d, y_table[2 * width:])
            old = inner[2 * z, here, :]
            inner[2 * z, here, :] = jnp.where(mark, old + values, old)

    column = from_right[:, from_right.shape[1] - fine:].T
    lane = lax.broadcasted_iota(jnp.int32, (fine, lanes), 1)
    last = (lane == lanes - 1) & (at == pl.num_programs(0) - 1)
    for k in range(planes):
        out[k] = jnp.where(last, w[k] - 0.5 * column[:, k:k + 1], w[k])
    even_lane = lax.broadcasted_iota(jnp.int32, (n, lanes), 1) % 2 == 0
    for z in range(half):
        wide = dot(inner[z], spread[...])
        here = (2 * z, pl.ds(0, n, stride=2), slice(None))
        out[here] = jnp.where(even_lane, wide, out[here])


def shards(density):
    planes, fine, width = density.shape
    half, n = planes // 2, fine // 2
    depth = min(64, fine)
    z_a, z_d = z_tables(planes)
    z2_a, z2_d = z_tables(half)
    (own_a, own_d), send, x_receive, x_level2 = x_tables(fine)
    y_table, y_receive, y_level2, y_spread = y_tables(width)
    rows = n + 8
    left = np.concatenate([part[:, :depth] for part in send[0]], 1)
    right = np.concatenate([part[:, fine - depth:] for part in send[1]], 1)
    as32 = lambda table: jnp.asarray(table, F32)
    params = pltpu.CompilerParams(vmem_limit_bytes=48 * 2**20)
    smem = pl.BlockSpec(memory_space=pltpu.SMEM)
    vmem = pl.BlockSpec(memory_space=pltpu.VMEM)
    shape = lambda *dims: jax.ShapeDtypeStruct(dims, F32)
    parity_x, parity_y = parity_of("gx"), parity_of("gy")

    to_inner, to_outer = pl.pallas_call(
        functools.partial(edge_kernel, z_a, z_d),
        out_shape=(shape(16, half * width),) * 2,
        grid=(1,),
        in_specs=[
            smem,
            pl.BlockSpec((planes, depth, width), lambda i: (0, 0, 0)),
            pl.BlockSpec((planes, depth, width), lambda i: (0, fine // depth - 1, 0)),
            vmem, vmem,
        ],
        out_specs=[vmem, vmem],
        compiler_params=params,
        name="edges",
    )(parity_x, density, density, as32(left), as32(right))
    inner_x, outer_x = swap(to_inner, to_outer, "gx")

    c_own, column = pl.pallas_call(
        functools.partial(own_kernel, z_a, z_d),
        out_shape=(shape(half, rows, width), shape(planes, fine)),
        grid=(1,),
        in_specs=[
            pl.BlockSpec((planes, fine, width // 2), lambda i: (0, 0, 0)),
            pl.BlockSpec((planes, fine, width // 2), lambda i: (0, 0, 1)),
        ] + [vmem] * 3,
        out_specs=[vmem] * 2,
        compiler_params=params,
        name="own",
    )(density, density, as32(own_a), as32(own_d), as32(y_table))

    c, message = pl.pallas_call(
        join_kernel,
        out_shape=(shape(half, rows, width), shape(8, half * 384 + fine)),
        in_specs=[smem] + [vmem] * 6,
        out_specs=[vmem] * 2,
        compiler_params=params,
        name="join",
    )(parity_x, c_own, column, inner_x, outer_x, as32(x_receive), as32(y_table))
    inner_y, outer_y = swap(message, message, "gy")

    w = pl.pallas_call(
        detail_kernel,
        out_shape=shape(planes, fine, width),
        in_specs=[smem] + [vmem] * 3,
        out_specs=vmem,
        compiler_params=params,
        name="details",
    )(parity_x, density, inner_x, outer_x)

    return pl.pallas_call(
        functools.partial(last_kernel, z2_a, z2_d),
        out_shape=shape(planes, fine, width),
        grid=(width // 128,),
        in_specs=[
            smem,
            vmem,
            pl.BlockSpec((planes, fine, 128), lambda i: (0, 0, i)),
            vmem, vmem, vmem, vmem, vmem,
            pl.BlockSpec((width // 2, 128), lambda i: (0, i)),
        ],
        out_specs=pl.BlockSpec((planes, fine, 128), lambda i: (0, 0, i)),
        scratch_shapes=[pltpu.VMEM((half, n, width // 2), F32)],
        compiler_params=params,
        name="last",
    )(parity_y, c, w, inner_y, outer_y, as32(y_receive), as32(x_level2), as32(y_level2), as32(y_spread))


def solution(mesh):
    spec = P(None, "gx", "gy")
    return jax.shard_map(shards, mesh=mesh, in_specs=(spec,), out_specs=spec, check_vma=False)
```

```python
import functools

import jax
import jax.numpy as jnp
import numpy as np
from jax import lax
from jax.experimental import pallas as pl
from jax.experimental.pallas import tpu as pltpu
from jax.sharding import PartitionSpec as P

ROOT = np.sqrt(3.0) - 2.0
CENTRE = 3.0 / np.sqrt(12.0)
F32 = jnp.float32


def line_operators(fine):
    n = fine // 2
    load = np.zeros((3 * n, 3 * fine))
    even = np.zeros((3 * n, 3 * n))
    for j in range(3 * n):
        for at, weight in ((2 * j, 1 / 3), (2 * j - 2, -1 / 6), (2 * j + 2, -1 / 6),
                           (2 * j - 1, 0.5), (2 * j + 1, 0.5)):
            if 0 <= at < 3 * fine:
                load[j, at] = weight
        for at, weight in ((j, 5 / 6), (j - 1, 1 / 12), (j + 1, 1 / 12)):
            if 0 <= at < 3 * n:
                even[j, at] = weight
    place = np.arange(3 * n)
    solve = CENTRE * ROOT ** np.abs(place[:, None] - place[None, :])
    a = (solve @ load)[:, fine:2 * fine]
    d = (solve @ even)[:, n:2 * n]
    near = np.arange(n)
    return dict(
        n=n, a=a[n:2 * n], a_left=a[n - 1], a_right=a[2 * n],
        d=d[n:2 * n], d_left=d[n - 1], d_right=d[2 * n],
        from_left=ROOT ** near, from_right=ROOT ** (n - 1 - near),
    )


def on_even(rows):
    wide = np.zeros(rows.shape[:-1] + (2 * rows.shape[-1],))
    wide[..., ::2] = rows
    return wide


def two_levels(fine):
    one = line_operators(fine)
    two = line_operators(one["n"])
    functionals = dict(
        a_left=two["a_left"], a_right=two["a_right"],
        d_left=on_even(two["d_left"]), d_right=on_even(two["d_right"]),
    )
    return one, two, functionals


def pieces(table, axis):
    high = table.astype(jnp.bfloat16)
    low = (table - high.astype(np.float64)).astype(jnp.bfloat16)
    return np.concatenate([high, low, high], axis)


def cut(data, axis):
    high = data.astype(jnp.bfloat16)
    low = (data - high.astype(F32)).astype(jnp.bfloat16)
    return jnp.concatenate([high, high, low], axis)


def dot(a, b, dims=((1,), (0,))):
    return lax.dot_general(a, b, (dims, ((), ())), preferred_element_type=F32)


def x_tables(fine):
    one, two, f = two_levels(fine)
    n = one["n"]
    rows = n + 16
    own = []
    for kind in ("a", "d"):
        table = np.zeros((rows, one[kind].shape[1]))
        left, right = one[kind + "_left"], one[kind + "_right"]
        table[:n] = one[kind]
        table[n] = right
        table[n + 1] = (f["a_right"] @ one["from_right"]) * left
        table[n + 2] = (f["a_left"] @ one["from_left"]) * right
        table[n + 3] = (f["d_right"] @ one["from_right"]) * left
        table[n + 4] = (f["d_left"] @ one["from_left"]) * right
        own.append(table)
    send = []
    for side in ("left", "right"):
        part = np.zeros((16, fine))
        for base, step, kind in ((0, 1, "a"), (4, 2, "d")):
            part[base, ::step] = one[kind + "_" + side]
            part[base + 1, ::step] = f["a_" + side] @ one[kind]
            part[base + 2, ::step] = f["d_" + side] @ one[kind]
            part[base + 3, ::step] = one[kind][0]
        part[8], part[9] = on_even(f["a_" + side]), on_even(f["d_" + side])
        send.append(part)
    receive = np.zeros((rows, 32))
    for base in (0, 4):
        receive[:n, base] = one["from_left"]
        receive[n + 1, base + 1] = 1
        receive[n + 3, base + 2] = 1
        receive[:n, 16 + base] = one["from_right"]
        receive[n + 2, 16 + base + 1] = 1
        receive[n + 4, 16 + base + 2] = 1
        receive[n, 16 + base + 3] = 1
    receive[n + 1, 8] = receive[n + 3, 9] = 1
    receive[n + 2, 16 + 8] = receive[n + 4, 16 + 9] = receive[n, 16 + 10] = 1
    m = n // 2
    level2_a, level2_d = np.zeros((m, rows)), np.zeros((m, rows))
    level2_a[:, :n], level2_d[:, :n] = two["a"], on_even(two["d"])
    level2_a[:, n + 1], level2_a[:, n + 2] = two["from_left"], two["from_right"]
    level2_d[:, n + 3], level2_d[:, n + 4] = two["from_left"], two["from_right"]
    return own, send, receive, level2_a, level2_d


SENT = dict(zip(("left", "right", "a_left", "a_right", "d_left", "d_right", "first"),
                (9, 1, 11, 3, 13, 5, 15)))
MESSAGE_ROW = dict(zip(SENT, range(7)))
MOMENTS = (17, 19, 21, 23)


def y_tables(fine):
    one, two, f = two_levels(fine)
    n = one["n"]

    def fill(table, inside, left, right):
        table[:, ::2] = inside.T
        table[:, fine - 1] = right
        table[:, MOMENTS[0]] = (f["a_right"] @ one["from_right"]) * left
        table[:, MOMENTS[1]] = (f["a_left"] @ one["from_left"]) * right
        table[:, MOMENTS[2]] = (f["d_right"] @ one["from_right"]) * left
        table[:, MOMENTS[3]] = (f["d_left"] @ one["from_left"]) * right
        table[:, SENT["left"]], table[:, SENT["right"]] = left, right
        for name in ("a_left", "a_right", "d_left", "d_right"):
            table[:, SENT[name]] = f[name] @ inside
        table[:, SENT["first"]] = inside[0]
        return table

    a = fill(np.zeros((fine, fine)), one["a"], one["a_left"], one["a_right"])
    d = fill(np.zeros((n, fine)), one["d"], one["d_left"], one["d_right"])
    e = fill(np.zeros((n, fine)), np.eye(n), np.zeros(n), np.zeros(n))
    e[:, ::2] = 0
    both = np.zeros((fine, fine))
    both[::2], both[1::2] = -d, e
    receive = np.zeros((16, fine))
    at = MESSAGE_ROW
    receive[at["right"], ::2] = one["from_left"]
    receive[at["a_right"], MOMENTS[0]] = receive[at["d_right"], MOMENTS[2]] = 1
    receive[8 + at["left"], ::2] = one["from_right"]
    receive[8 + at["a_left"], MOMENTS[1]] = receive[8 + at["d_left"], MOMENTS[3]] = 1
    receive[8 + at["first"], fine - 1] = 1
    level2_a, level2_d = np.zeros((fine, n // 2)), np.zeros((fine, n // 2))
    level2_a[::2], level2_d[::2] = two["a"].T, -on_even(two["d"]).T
    level2_a[MOMENTS[0]], level2_a[MOMENTS[1]] = two["from_left"], two["from_right"]
    level2_d[MOMENTS[2]], level2_d[MOMENTS[3]] = -two["from_left"], -two["from_right"]
    level2_a, level2_d = on_even(on_even(level2_a)), on_even(on_even(level2_d))
    predict = np.zeros((fine, fine))
    for j in range(0, fine, 2):
        predict[j, j] = 1
        if j % 4:
            predict[j - 2, j] = predict[(j + 2) if j + 2 < fine else fine - 1, j] = -0.5
    updates = [receive @ predict, receive @ level2_a, receive @ level2_d]
    return a, both, level2_a, level2_d, updates


def z_tables(planes):
    n = planes // 2
    predict, spread = np.eye(planes), np.zeros((planes, n))
    mass, restrict, solve = (np.zeros(s) for s in ((planes, planes), (n, planes), (n, n)))
    for i in range(planes):
        for at, weight in ((i, 4 / 6), (i - 1, 1 / 6), (i + 1, 1 / 6)):
            mass[i, at % planes] += weight
        if i % 2:
            predict[i, i - 1] -= 0.5
            predict[i, (i + 1) % planes] -= 0.5
    for j in range(n):
        spread[2 * j, j] = 1
        for at, weight in ((2 * j, 1.0), (2 * j - 1, 0.5), (2 * j + 1, 0.5)):
            restrict[j, at % planes] += weight
        for at, weight in ((j, 4 / 3), (j - 1, 1 / 3), (j + 1, 1 / 3)):
            solve[j, at % n] += weight
    load = np.linalg.inv(solve) @ restrict @ mass
    return (load @ predict).tolist(), (load @ spread).tolist()


def pack(arrays, width):
    blocks, places, start = [], [], 0
    for array in arrays:
        rows, columns = array.shape
        count = -(-columns // width)
        padded = np.pad(array, ((0, 0), (0, count * width - columns)))
        blocks += [padded[:, k * width:(k + 1) * width] for k in range(count)]
        places.append((start, rows, columns))
        start += rows * count
    return np.concatenate(blocks, 0), tuple(places)


def unpack(table, place):
    start, rows, columns = place
    width = table.shape[1]
    count = -(-columns // width)
    blocks = [table[start + k * rows:start + (k + 1) * rows, :] for k in range(count)]
    whole = blocks[0] if count == 1 else jnp.concatenate(blocks, 1)
    return whole if columns == count * width else whole[:, :columns]


def combine(weights, planes):
    total = None
    for weight, plane in zip(weights, planes):
        term = plane * float(weight)
        total = term if total is None else total + term
    return total


def exchange(to_left, to_right, axis):
    size = lax.axis_size(axis)
    forward = [(i, (i + 1) % size) for i in range(size)]
    backward = [(target, source) for source, target in forward]
    right = lax.ppermute(to_left, axis, backward)
    return lax.ppermute(to_right, axis, forward), right


def iota(shape, dimension):
    return lax.broadcasted_iota(jnp.int32, shape, dimension)


def edge_weights(table, shape, reverse):
    near = table[:, ::-1] if reverse else table
    row, lane = iota(shape, 0), iota(shape, 1)
    place = (shape[1] - 1 - lane) if reverse else lane
    group = place // 4
    sign = jnp.where(group % 2 == 1, -1.0, 1.0)
    one = jnp.exp(group.astype(F32) * float(np.log(-ROOT)))
    slow, fast = sign * one, one * one
    total = jnp.zeros(shape, F32)
    for phase in range(4):
        some = near[:, phase::4]
        basis = np.stack([ROOT ** np.arange(1, 5), ROOT ** (2 * np.arange(1, 5))], 1)
        factors = np.linalg.lstsq(basis, some[:, 1:5].T, rcond=None)[0]
        here = place % 4 == phase
        first = jnp.zeros(shape, F32)
        rest_slow, rest_fast = jnp.zeros(shape, F32), jnp.zeros(shape, F32)
        for k in range(table.shape[0]):
            if np.any(some[k]):
                mine = row == k
                first = jnp.where(mine, float(some[k, 0]), first)
                rest_slow = jnp.where(mine, float(factors[0, k]), rest_slow)
                rest_fast = jnp.where(mine, float(factors[1, k]), rest_fast)
        rest = rest_slow * slow + rest_fast * fast
        total = jnp.where(here, jnp.where(group == 0, first, rest), total)
    return total


def edge_kernel(tables, z_a, z_d, u, to_left, to_right, strips, arrived):
    _, planes, halves, depth, lanes = strips.shape
    fine = u.shape[1]
    copies = [
        [
            pltpu.make_async_copy(
                u.at[:, pl.ds(start, depth), pl.ds(h * lanes, lanes)],
                strips.at[side, :, h],
                arrived.at[side, h],
            )
            for h in range(halves)
        ]
        for side, start in ((0, 0), (1, fine - depth))
    ]
    for band in copies:
        for copy in band:
            copy.start()
    weights = []
    for side in range(2):
        weight = edge_weights(tables[side], (16, depth), side == 1)
        high = weight.astype(jnp.bfloat16)
        low = (weight - high.astype(F32)).astype(jnp.bfloat16)
        weights.append(jnp.concatenate([high, low, high], 1))

    def message(side):
        for copy in copies[side]:
            copy.wait()
        tiles = [strips[side, k, h] for k in range(planes) for h in range(halves)]
        data = jnp.concatenate(tiles, 1)
        width = halves * lanes
        sums = dot(weights[side], cut(data, 0))
        plane = [sums[:, k * width:(k + 1) * width] for k in range(planes)]
        index = iota(plane[0].shape, 0)
        out = []
        for z in range(planes // 2):
            a, d = combine(z_a[z], plane), combine(z_d[z], plane[::2])
            part = jnp.where(index < 4, a, jnp.where(index < 8, d, plane[2 * z]))
            if side == 0:
                even = data[:1, 2 * z * width:(2 * z + 1) * width]
                odd = data[:1, (2 * z + 1) * width:(2 * z + 2) * width]
                part = jnp.where(index == 10, even, jnp.where(index == 11, odd, part))
            out.append(part)
        return jnp.concatenate(out, 1)

    to_left[...] = message(0)
    to_right[...] = message(1)


def own_kernel(z_a, z_d, reach, places, block, table, c, side, column, u, arrived):
    planes, halves, fine, lanes = u.shape
    part = fine // 2
    copies = [
        [
            pltpu.make_async_copy(
                block.at[:, pl.ds(at * part, part), pl.ds(h * lanes, lanes)],
                u.at[:, h, pl.ds(at * part, part), :],
                arrived.at[at, h],
            )
            for h in range(halves)
        ]
        for at in range(2)
    ]
    for some in copies:
        for copy in some:
            copy.start()
    n, rows, stride = fine // 2, c.shape[1], side.shape[1] // c.shape[0]
    join = lambda parts: jnp.concatenate(parts, 1)
    tables = [unpack(table, place) for place in places]
    y_table = tables[4]
    even, x_parts = [], []
    for at in range(2):
        for copy in copies[at]:
            copy.wait()
        whole = [
            join([u[k, h, at * part:(at + 1) * part, :] for h in range(halves)])
            for k in range(planes)
        ]
        even.append([
            join([u[k, h, pl.ds(at * part, part // 2, stride=2), :] for h in range(halves)])
            for k in range(0, planes, 2)
        ])
        x_parts.append([
            [
                dot(tables[2 * at], cut(combine(z_a[z], whole), 0)),
                dot(tables[2 * at + 1], cut(combine(z_d[z], even[at]), 0)),
            ]
            for z in range(planes // 2)
        ])

    def whole_rows(low, high):
        middle, edge = n // 2 - reach, n // 2 + reach
        return jnp.concatenate([
            low[:middle], low[middle:edge] + high[:2 * reach], high[2 * reach:edge],
            low[edge:] + high[edge:],
        ], 0)

    for z in range(planes // 2):
        x_a = whole_rows(x_parts[0][z][0], x_parts[1][z][0])
        x_d = whole_rows(x_parts[0][z][1], x_parts[1][z][1])
        odd_lane = iota(x_d.shape, 1) % 2 == 1
        field = jnp.concatenate([even[0][z], even[1][z], jnp.zeros((rows - n, halves * lanes), F32)], 0)
        x_de = jnp.where(odd_lane, pltpu.roll(field, 1, 1), x_d)
        total = dot(join([cut(x_a, 1), cut(x_de, 1)]), y_table)
        total = total + jnp.where(odd_lane, 0.0, field)
        c[z] = total
        turned = total[:, :lanes].T
        index = iota((8, rows), 0)
        kept = jnp.where(index % 2 == 1, turned[:8], pltpu.roll(turned[8:16], 7, 0))
        side[:, z * stride:z * stride + rows] = kept
        if stride > rows:
            side[:, z * stride + rows:(z + 1) * stride] = jnp.zeros((8, stride - rows), F32)
    for k in range(planes):
        column[k:k + 1, :] = u[k, 0].T[:1, :]


def typed_rows(from_left, from_right, half):
    both = jnp.concatenate([from_left, from_right], 0)
    width = both.shape[1] // half
    rows = jnp.concatenate([both[:, z * width:(z + 1) * width] for z in range(half)], 0)
    kind = iota(rows.shape, 0) % 16
    even_lane = iota(rows.shape, 1) % 2 == 0
    field = jnp.where((kind >= 8) & (kind <= 10) & even_lane, rows, 0.0)
    a = jnp.where(kind < 4, rows, 0.0)
    d = jnp.where((kind >= 4) & (kind < 8) & even_lane, rows, 0.0)
    return jnp.concatenate([cut(a, 1), cut(d + pltpu.roll(field, 1, 1), 1)], 1), field


def join_kernel(half, side, column, left, right, y_sent, receive, message, again):
    from_left, from_right = left[...], right[...]
    typed, _ = typed_rows(from_left, from_right, half)
    sums = dot(y_sent[...], typed, ((1,), (1,)))[:8]
    part = iota(sums.shape, 1) // 32
    spread = jnp.concatenate([jnp.where(part == z, sums, 0.0) for z in range(half)], 0)
    added = dot(cut(spread, 1), receive[...])
    stride = side.shape[1] // half
    for z in range(half):
        here = slice(z * stride, (z + 1) * stride)
        message[:, here] = side[:, here] + added[8 * z:8 * z + 8]
    u0 = column[...]
    fine = u0.shape[1]
    width = from_right.shape[1] // half
    plane, lane = iota(u0.shape, 0), iota(u0.shape, 1)
    after = pltpu.roll(u0, fine - 1, 1)
    for z in range(half):
        for k, row in ((2 * z, 10), (2 * z + 1, 11)):
            corner = from_right[row:row + 1, z * width:z * width + 1]
            after = jnp.where((plane == k) & (lane == fine - 1), corner, after)
    before = pltpu.roll(u0, 1, 1)
    u0 = jnp.where(lane % 2 == 1, u0 - 0.5 * (before + after), u0)
    around = pltpu.roll(u0, 1, 0) + pltpu.roll(u0, 2 * half - 1, 0)
    message[:, half * stride:] = jnp.where(plane % 2 == 1, u0 - 0.5 * around, u0)
    again[...] = message[...]


def middle_kernel(
    z_a, z_d, places, c_own, block, left, right, table, out, w, edge, u, inner, ready, arrived, sent
):
    planes, halves, fine, lanes = u.shape
    copies = [
        pltpu.make_async_copy(block.at[:, :, pl.ds(h * lanes, lanes)], u.at[:, h], arrived.at[h])
        for h in range(halves)
    ]
    for copy in copies:
        copy.start()
    half, rows, width = c_own.shape
    n, quarter = fine // 2, fine // 4
    from_left, from_right = left[...], right[...]
    typed, field = typed_rows(from_left, from_right, half)
    y_table, receive, x_level2, y_level2 = (unpack(table, place) for place in places)
    processed = dot(typed, y_table) + field
    lane = iota((rows, width), 1)
    row = iota((rows, width), 0)
    coarse, details = [], []
    for z in range(half):
        c = c_own[z] + dot(receive, cut(processed[32 * z:32 * z + 32], 0))
        coarse.append(c)
        around = pltpu.roll(c, 1, 0) + pltpu.roll(c, rows - 1, 0)
        c = jnp.where(row % 2 == 1, c - 0.5 * around, c)[:n]
        after = pltpu.roll(c, width - 2, 1)
        after = jnp.where(lane[:n] == width - 2, pltpu.roll(c, width - 1, 1), after)
        around = pltpu.roll(c, 2, 1) + after
        details.append(jnp.where(lane[:n] % 4 == 2, c - 0.5 * around, c))
    level = [dot(x_level2, cut(c, 0)) for c in coarse]
    level_a = [part[:quarter] for part in level]
    level_d = [part[quarter:] for part in level[::2]]
    for z in range(half):
        values = details[z]
        if z % 2:
            values = values - 0.5 * (details[z - 1] + details[(z + 1) % half])
        for h in range(halves):
            inner[z, h] = values[:, h * lanes:(h + 1) * lanes]
        if z % 2 == 0:
            a, d = combine(z_a[z // 2], level_a), combine(z_d[z // 2], level_d)
            added = dot(jnp.concatenate([cut(a, 1), cut(d, 1)], 1), y_level2)
            for h in range(halves):
                here = (z, h, pl.ds(0, quarter, stride=2), slice(None))
                inner[here] = inner[here] + added[:, h * lanes:(h + 1) * lanes]

    for copy in copies:
        copy.wait()
    last_row = iota((n, width), 0) == n - 1
    even_lane = iota((n, width), 1) % 2 == 0

    def rows_of(k):
        load = lambda start: jnp.concatenate(
            [u[k, h, pl.ds(start, n, stride=2), :] for h in range(halves)], 1
        )
        even, odd = load(0), load(1)
        at = (k // 2) * width
        halo = from_right[10 + k % 2:11 + k % 2, at:at + width]
        after = jnp.where(last_row, halo, pltpu.roll(even, n - 1, 0))
        return even, odd - 0.5 * (even + after)

    def along_y(part):
        after = jnp.where(iota(part.shape, 1) == width - 1, 0.0, pltpu.roll(part, width - 1, 1))
        return jnp.where(even_lane, part, part - 0.5 * (pltpu.roll(part, 1, 1) + after))

    def store(k, start, part):
        for h in range(halves):
            target = w.at[k // 2, h] if k % 2 == 0 else (
                edge.at[k // 2] if h == halves - 1 else ready.at[k // 2, h])
            target[pl.ds(start, n, stride=2), :] = part[:, h * lanes:(h + 1) * lanes]

    begin = rows_of(0)
    here, done = begin, []
    for k in range(0, planes, 2):
        held = jnp.concatenate([inner[k // 2, h] for h in range(halves)], 1)
        store(k, 0, jnp.where(even_lane, held, along_y(here[0])))
        store(k, 1, along_y(here[1]))
        following = begin if k + 2 == planes else rows_of(k + 2)
        between = rows_of(k + 1)
        for start in (0, 1):
            store(k + 1, start, along_y(between[start] - 0.5 * (here[start] + following[start])))
        for h in range(halves - 1):
            copy = pltpu.make_async_copy(
                ready.at[k // 2, h], out.at[k + 1, :, pl.ds(h * lanes, lanes)], sent.at[k // 2, h]
            )
            copy.start()
            done.append(copy)
        here = following
    for copy in done:
        copy.wait()


def last_kernel(
    z_a, z_d, left, right, x_level2, updates, w, edge, started, out, done, finished, sent
):
    half, halves, fine, lanes = w.shape
    n = fine // 2
    stride = (left.shape[1] - fine) // half
    from_left, from_right = left[...], right[...]
    column = from_right[:, half * stride:].T
    last = iota((fine, lanes), 1) == lanes - 1
    copies = []

    def send(source, k, h):
        copy = pltpu.make_async_copy(source, out.at[k, :, pl.ds(h * lanes, lanes)], sent.at[k, h])
        copy.start()
        copies.append(copy)

    def finish(values, k):
        return jnp.where(last, values - 0.5 * column[:, k:k + 1], values)

    for z in range(half):
        finished[z] = finish(edge[z], 2 * z + 1)
        send(finished.at[z], 2 * z + 1, halves - 1)
        for h in range(halves):
            done[z, h] = finish(w[z, h], 2 * z) if h == halves - 1 else w[z, h]
    both = jnp.concatenate([from_left, from_right], 0)
    sides = [both[:, z * stride:(z + 1) * stride] for z in range(half)]
    level = dot(cut(jnp.concatenate(sides, 0), 1), x_level2[...])
    lane = iota(sides[0].shape, 1)
    details = []
    for side in sides:
        around = pltpu.roll(side, 1, 1) + pltpu.roll(side, stride - 1, 1)
        details.append(jnp.where(lane % 2 == 1, side - 0.5 * around, side)[:, :n])
    quarter = n // 2
    level_a = [level[16 * z:16 * z + 16, :quarter] for z in range(half)]
    level_d = [level[16 * z:16 * z + 16, quarter:] for z in range(0, half, 2)]

    def update(factor, start):
        stop = start + factor.shape[0]
        table = jnp.concatenate([updates[piece, start:stop] for piece in range(3)], 0)
        return dot(cut(factor, 0), table, ((0,), (0,)))

    for z in range(half):
        if z % 2:
            factor = details[z] - 0.5 * (details[z - 1] + details[(z + 1) % half])
        else:
            factor = details[z]
            parts = [combine(z_a[z // 2], level_a), combine(z_d[z // 2], level_d)]
            coarse = update(jnp.concatenate(parts, 0), 16)
        added = update(factor, 0)
        for h in range(halves):
            here = (z, h, pl.ds(0, n, stride=2), slice(None))
            done[here] = done[here] + added[:, h * lanes:(h + 1) * lanes]
            if z % 2 == 0:
                here = (z, h, pl.ds(0, quarter, stride=4), slice(None))
                done[here] = done[here] + coarse[:, h * lanes:(h + 1) * lanes]
            send(done.at[z, h], 2 * z, h)
    for copy in copies:
        copy.wait()


def shards(density):
    planes, fine, width = density.shape
    half, n, lanes = planes // 2, fine // 2, 128
    halves = width // lanes
    depth = min(64, fine)
    z_a, z_d = z_tables(planes)
    z2_a, z2_d = z_tables(half)
    (own_a, own_d), send, x_receive, x2_a, x2_d = x_tables(fine)
    y_a, y_de, y2_a, y2_d, updates = y_tables(width)
    rows = n + 16
    stride = -(-rows // 128) * 128
    y_table = np.concatenate([pieces(y_a, 0), pieces(y_de, 0)], 0)
    sent = list(SENT.values())
    y_sent = np.zeros((16, y_table.shape[0]), y_table.dtype)
    y_sent[:len(sent)] = y_table[:, sent].T
    x_receive_t = np.zeros((32, stride))
    x_receive_t[:, :rows] = x_receive.T
    x2_t = np.zeros((stride, n))
    x2_t[:rows] = np.concatenate([x2_a.T, x2_d.T], 1)
    update = np.concatenate(updates, 0)
    high = update.astype(jnp.bfloat16)
    low = (update - high.astype(np.float64)).astype(jnp.bfloat16)
    params = lambda mib: pltpu.CompilerParams(vmem_limit_bytes=mib * 2**20)
    vmem = pl.BlockSpec(memory_space=pltpu.VMEM)
    hbm = pl.BlockSpec(memory_space=pltpu.HBM)
    shape = lambda *dims: jax.ShapeDtypeStruct(dims, F32)

    to_left, to_right = pl.pallas_call(
        functools.partial(edge_kernel, (send[0][:, :depth], send[1][:, fine - depth:]), z_a, z_d),
        out_shape=(shape(16, half * width),) * 2,
        in_specs=[hbm],
        out_specs=[vmem] * 2,
        scratch_shapes=[
            pltpu.VMEM((2, planes, halves, depth, lanes), F32),
            pltpu.SemaphoreType.DMA((2, halves)),
        ],
        compiler_params=params(50),
        name="edges",
    )(density)
    left_x, right_x = exchange(to_left, to_right, "gx")

    reach = min(16, n // 2)
    tail = list(range(n, rows))
    front = list(range(n // 2 + reach)) + tail
    back = list(range(n // 2 - reach, n)) + tail
    packed, places = pack(
        [
            pieces(own_a[front][:, :n], 1), pieces(own_d[front][:, :n // 2], 1),
            pieces(own_a[back][:, n:], 1), pieces(own_d[back][:, n // 2:], 1),
            y_table,
        ],
        width,
    )
    c_own, side, column = pl.pallas_call(
        functools.partial(own_kernel, z_a, z_d, reach, places),
        out_shape=(shape(half, rows, width), shape(8, half * stride), shape(planes, fine)),
        in_specs=[hbm, vmem],
        out_specs=[vmem] * 3,
        scratch_shapes=[
            pltpu.VMEM((planes, halves, fine, lanes), F32),
            pltpu.SemaphoreType.DMA((2, halves)),
        ],
        compiler_params=params(50),
        name="own",
    )(density, packed)

    to_left, to_right = pl.pallas_call(
        functools.partial(join_kernel, half),
        out_shape=(shape(8, half * stride + fine),) * 2,
        in_specs=[vmem] * 6,
        out_specs=[vmem] * 2,
        compiler_params=params(8),
        name="join",
    )(side, column, left_x, right_x, y_sent, pieces(np.tile(x_receive_t, (half, 1)), 0))
    left_y, right_y = exchange(to_left, to_right, "gy")

    x_level2 = pieces(np.concatenate([x2_a, x2_d], 0), 1)
    y_level2 = np.concatenate([pieces(y2_a, 0), pieces(y2_d, 0)], 0)
    packed, places = pack([y_table, pieces(x_receive, 1), x_level2, y_level2], width)
    started, w, edge = pl.pallas_call(
        functools.partial(middle_kernel, z2_a, z2_d, places),
        out_shape=(
            shape(planes, fine, width), shape(half, halves, fine, lanes), shape(half, fine, lanes),
        ),
        in_specs=[vmem, hbm, vmem, vmem, vmem],
        out_specs=[hbm, vmem, vmem],
        scratch_shapes=[
            pltpu.VMEM((planes, halves, fine, lanes), F32),
            pltpu.VMEM((half, halves, n, lanes), F32),
            pltpu.VMEM((half, halves - 1, fine, lanes), F32),
            pltpu.SemaphoreType.DMA((halves,)),
            pltpu.SemaphoreType.DMA((half, halves - 1)),
        ],
        compiler_params=params(44),
        name="middle",
    )(c_own, density, left_x, right_x, packed)

    return pl.pallas_call(
        functools.partial(last_kernel, z2_a, z2_d),
        out_shape=shape(planes, fine, width),
        in_specs=[vmem] * 6 + [hbm],
        out_specs=hbm,
        scratch_shapes=[
            pltpu.VMEM((half, halves, fine, lanes), F32),
            pltpu.VMEM((half, fine, lanes), F32),
            pltpu.SemaphoreType.DMA((planes, halves)),
        ],
        input_output_aliases={6: 0},
        compiler_params=params(16),
        name="last",
    )(left_y, right_y, pieces(x2_t, 0), np.stack([high, low, high]), w, edge, started)


def solution(mesh):
    spec = P(None, "gx", "gy")
    return jax.shard_map(shards, mesh=mesh, in_specs=(spec,), out_specs=spec, check_vma=False)
```

```python
import functools

import jax
import jax.numpy as jnp
import numpy as np
from jax import lax
from jax.experimental import pallas as pl
from jax.experimental.pallas import tpu as pltpu
from jax.sharding import PartitionSpec as P

ROOT = np.sqrt(3.0) - 2.0
CENTRE = 3.0 / np.sqrt(12.0)
F32 = jnp.float32


def line_operators(fine):
    n = fine // 2
    load = np.zeros((3 * n, 3 * fine))
    even = np.zeros((3 * n, 3 * n))
    for j in range(3 * n):
        for at, weight in ((2 * j, 1 / 3), (2 * j - 2, -1 / 6), (2 * j + 2, -1 / 6),
                           (2 * j - 1, 0.5), (2 * j + 1, 0.5)):
            if 0 <= at < 3 * fine:
                load[j, at] = weight
        for at, weight in ((j, 5 / 6), (j - 1, 1 / 12), (j + 1, 1 / 12)):
            if 0 <= at < 3 * n:
                even[j, at] = weight
    place = np.arange(3 * n)
    solve = CENTRE * ROOT ** np.abs(place[:, None] - place[None, :])
    a = (solve @ load)[:, fine:2 * fine]
    d = (solve @ even)[:, n:2 * n]
    near = np.arange(n)
    return dict(
        n=n, a=a[n:2 * n], a_left=a[n - 1], a_right=a[2 * n],
        d=d[n:2 * n], d_left=d[n - 1], d_right=d[2 * n],
        from_left=ROOT ** near, from_right=ROOT ** (n - 1 - near),
    )


def on_even(rows):
    wide = np.zeros(rows.shape[:-1] + (2 * rows.shape[-1],))
    wide[..., ::2] = rows
    return wide


def two_levels(fine):
    one = line_operators(fine)
    two = line_operators(one["n"])
    functionals = dict(
        a_left=two["a_left"], a_right=two["a_right"],
        d_left=on_even(two["d_left"]), d_right=on_even(two["d_right"]),
    )
    return one, two, functionals


def pieces(table, axis):
    high = table.astype(jnp.bfloat16)
    low = (table - high.astype(np.float64)).astype(jnp.bfloat16)
    return np.concatenate([high, low, high], axis)


def cut(data, axis):
    high = data.astype(jnp.bfloat16)
    low = (data - high.astype(F32)).astype(jnp.bfloat16)
    return jnp.concatenate([high, high, low], axis)


def dot(a, b, dims=((1,), (0,))):
    return lax.dot_general(a, b, (dims, ((), ())), preferred_element_type=F32)


def x_tables(fine):
    one, two, f = two_levels(fine)
    n = one["n"]
    rows = n + 16
    own = []
    for kind in ("a", "d"):
        table = np.zeros((rows, one[kind].shape[1]))
        left, right = one[kind + "_left"], one[kind + "_right"]
        table[:n] = one[kind]
        table[n] = right
        table[n + 1] = (f["a_right"] @ one["from_right"]) * left
        table[n + 2] = (f["a_left"] @ one["from_left"]) * right
        table[n + 3] = (f["d_right"] @ one["from_right"]) * left
        table[n + 4] = (f["d_left"] @ one["from_left"]) * right
        own.append(table)
    send = []
    for side in ("left", "right"):
        part = np.zeros((16, fine))
        for base, step, kind in ((0, 1, "a"), (4, 2, "d")):
            part[base, ::step] = one[kind + "_" + side]
            part[base + 1, ::step] = f["a_" + side] @ one[kind]
            part[base + 2, ::step] = f["d_" + side] @ one[kind]
            part[base + 3, ::step] = one[kind][0]
        part[8], part[9] = on_even(f["a_" + side]), on_even(f["d_" + side])
        send.append(part)
    receive = np.zeros((rows, 32))
    for base in (0, 4):
        receive[:n, base] = one["from_left"]
        receive[n + 1, base + 1] = 1
        receive[n + 3, base + 2] = 1
        receive[:n, 16 + base] = one["from_right"]
        receive[n + 2, 16 + base + 1] = 1
        receive[n + 4, 16 + base + 2] = 1
        receive[n, 16 + base + 3] = 1
    receive[n + 1, 8] = receive[n + 3, 9] = 1
    receive[n + 2, 16 + 8] = receive[n + 4, 16 + 9] = receive[n, 16 + 10] = 1
    m = n // 2
    level2_a, level2_d = np.zeros((m, rows)), np.zeros((m, rows))
    level2_a[:, :n], level2_d[:, :n] = two["a"], on_even(two["d"])
    level2_a[:, n + 1], level2_a[:, n + 2] = two["from_left"], two["from_right"]
    level2_d[:, n + 3], level2_d[:, n + 4] = two["from_left"], two["from_right"]
    return own, send, receive, level2_a, level2_d


SENT = dict(zip(("left", "right", "a_left", "a_right", "d_left", "d_right", "first"),
                (9, 1, 11, 3, 13, 5, 15)))
MESSAGE_ROW = dict(zip(SENT, range(7)))
MOMENTS = (17, 19, 21, 23)


def y_tables(fine):
    one, two, f = two_levels(fine)
    n = one["n"]

    def fill(table, inside, left, right):
        table[:, ::2] = inside.T
        table[:, fine - 1] = right
        table[:, MOMENTS[0]] = (f["a_right"] @ one["from_right"]) * left
        table[:, MOMENTS[1]] = (f["a_left"] @ one["from_left"]) * right
        table[:, MOMENTS[2]] = (f["d_right"] @ one["from_right"]) * left
        table[:, MOMENTS[3]] = (f["d_left"] @ one["from_left"]) * right
        table[:, SENT["left"]], table[:, SENT["right"]] = left, right
        for name in ("a_left", "a_right", "d_left", "d_right"):
            table[:, SENT[name]] = f[name] @ inside
        table[:, SENT["first"]] = inside[0]
        return table

    a = fill(np.zeros((fine, fine)), one["a"], one["a_left"], one["a_right"])
    d = fill(np.zeros((n, fine)), one["d"], one["d_left"], one["d_right"])
    e = fill(np.zeros((n, fine)), np.eye(n), np.zeros(n), np.zeros(n))
    e[:, ::2] = 0
    both = np.zeros((fine, fine))
    both[::2], both[1::2] = -d, e
    receive = np.zeros((16, fine))
    at = MESSAGE_ROW
    receive[at["right"], ::2] = one["from_left"]
    receive[at["a_right"], MOMENTS[0]] = receive[at["d_right"], MOMENTS[2]] = 1
    receive[8 + at["left"], ::2] = one["from_right"]
    receive[8 + at["a_left"], MOMENTS[1]] = receive[8 + at["d_left"], MOMENTS[3]] = 1
    receive[8 + at["first"], fine - 1] = 1
    level2_a, level2_d = np.zeros((fine, n // 2)), np.zeros((fine, n // 2))
    level2_a[::2], level2_d[::2] = two["a"].T, -on_even(two["d"]).T
    level2_a[MOMENTS[0]], level2_a[MOMENTS[1]] = two["from_left"], two["from_right"]
    level2_d[MOMENTS[2]], level2_d[MOMENTS[3]] = -two["from_left"], -two["from_right"]
    level2_a, level2_d = on_even(on_even(level2_a)), on_even(on_even(level2_d))
    predict = np.zeros((fine, fine))
    for j in range(0, fine, 2):
        predict[j, j] = 1
        if j % 4:
            predict[j - 2, j] = predict[(j + 2) if j + 2 < fine else fine - 1, j] = -0.5
    updates = [receive @ predict, receive @ level2_a, receive @ level2_d]
    return a, both, level2_a, level2_d, updates


def z_tables(planes):
    n = planes // 2
    predict, spread = np.eye(planes), np.zeros((planes, n))
    mass, restrict, solve = (np.zeros(s) for s in ((planes, planes), (n, planes), (n, n)))
    for i in range(planes):
        for at, weight in ((i, 4 / 6), (i - 1, 1 / 6), (i + 1, 1 / 6)):
            mass[i, at % planes] += weight
        if i % 2:
            predict[i, i - 1] -= 0.5
            predict[i, (i + 1) % planes] -= 0.5
    for j in range(n):
        spread[2 * j, j] = 1
        for at, weight in ((2 * j, 1.0), (2 * j - 1, 0.5), (2 * j + 1, 0.5)):
            restrict[j, at % planes] += weight
        for at, weight in ((j, 4 / 3), (j - 1, 1 / 3), (j + 1, 1 / 3)):
            solve[j, at % n] += weight
    load = np.linalg.inv(solve) @ restrict @ mass
    return (load @ predict).tolist(), (load @ spread).tolist()


def pack(arrays, width):
    blocks, places, start = [], [], 0
    for array in arrays:
        rows, columns = array.shape
        count = -(-columns // width)
        padded = np.pad(array, ((0, 0), (0, count * width - columns)))
        blocks += [padded[:, k * width:(k + 1) * width] for k in range(count)]
        places.append((start, rows, columns))
        start += rows * count
    return np.concatenate(blocks, 0), tuple(places)


def unpack(table, place):
    start, rows, columns = place
    width = table.shape[1]
    count = -(-columns // width)
    blocks = [table[start + k * rows:start + (k + 1) * rows, :] for k in range(count)]
    whole = blocks[0] if count == 1 else jnp.concatenate(blocks, 1)
    return whole if columns == count * width else whole[:, :columns]


def combine(weights, planes):
    total = None
    for weight, plane in zip(weights, planes):
        term = plane * float(weight)
        total = term if total is None else total + term
    return total


def exchange(to_left, to_right, axis):
    size = lax.axis_size(axis)
    forward = [(i, (i + 1) % size) for i in range(size)]
    backward = [(target, source) for source, target in forward]
    right = lax.ppermute(to_left, axis, backward)
    return lax.ppermute(to_right, axis, forward), right


def iota(shape, dimension):
    return lax.broadcasted_iota(jnp.int32, shape, dimension)


def edge_weights(table, shape, reverse):
    near = table[:, ::-1] if reverse else table
    row, lane = iota(shape, 0), iota(shape, 1)
    place = (shape[1] - 1 - lane) if reverse else lane
    group = place // 4
    sign = jnp.where(group % 2 == 1, -1.0, 1.0)
    one = jnp.exp(group.astype(F32) * float(np.log(-ROOT)))
    slow, fast = sign * one, one * one
    total = jnp.zeros(shape, F32)
    for phase in range(4):
        some = near[:, phase::4]
        basis = np.stack([ROOT ** np.arange(1, 5), ROOT ** (2 * np.arange(1, 5))], 1)
        factors = np.linalg.lstsq(basis, some[:, 1:5].T, rcond=None)[0]
        here = place % 4 == phase
        first = jnp.zeros(shape, F32)
        rest_slow, rest_fast = jnp.zeros(shape, F32), jnp.zeros(shape, F32)
        for k in range(table.shape[0]):
            if np.any(some[k]):
                mine = row == k
                first = jnp.where(mine, float(some[k, 0]), first)
                rest_slow = jnp.where(mine, float(factors[0, k]), rest_slow)
                rest_fast = jnp.where(mine, float(factors[1, k]), rest_fast)
        rest = rest_slow * slow + rest_fast * fast
        total = jnp.where(here, jnp.where(group == 0, first, rest), total)
    return total


def edge_kernel(tables, z_a, z_d, u, to_left, to_right, strips, arrived):
    _, planes, halves, depth, lanes = strips.shape
    fine = u.shape[1]
    copies = [
        [
            pltpu.make_async_copy(
                u.at[:, pl.ds(start, depth), pl.ds(h * lanes, lanes)],
                strips.at[side, :, h],
                arrived.at[side, h],
            )
            for h in range(halves)
        ]
        for side, start in ((0, 0), (1, fine - depth))
    ]
    for band in copies:
        for copy in band:
            copy.start()
    weights = []
    for side in range(2):
        weight = edge_weights(tables[side], (16, depth), side == 1)
        high = weight.astype(jnp.bfloat16)
        low = (weight - high.astype(F32)).astype(jnp.bfloat16)
        weights.append(jnp.concatenate([high, low, high], 1))

    def message(side):
        for copy in copies[side]:
            copy.wait()
        tiles = [strips[side, k, h] for k in range(planes) for h in range(halves)]
        data = jnp.concatenate(tiles, 1)
        width = halves * lanes
        sums = dot(weights[side], cut(data, 0))
        plane = [sums[:, k * width:(k + 1) * width] for k in range(planes)]
        index = iota(plane[0].shape, 0)
        out = []
        for z in range(planes // 2):
            a, d = combine(z_a[z], plane), combine(z_d[z], plane[::2])
            part = jnp.where(index < 4, a, jnp.where(index < 8, d, plane[2 * z]))
            if side == 0:
                even = data[:1, 2 * z * width:(2 * z + 1) * width]
                odd = data[:1, (2 * z + 1) * width:(2 * z + 2) * width]
                part = jnp.where(index == 10, even, jnp.where(index == 11, odd, part))
            out.append(part)
        return jnp.concatenate(out, 1)

    to_left[...] = message(0)
    to_right[...] = message(1)


def own_kernel(z_a, z_d, reach, parts, places, block, table, c, side, column, u, arrived):
    planes, halves, fine, lanes = u.shape
    size = fine // parts
    copies = [
        [
            pltpu.make_async_copy(
                block.at[:, pl.ds(at * size, size), pl.ds(h * lanes, lanes)],
                u.at[:, h, pl.ds(at * size, size), :],
                arrived.at[at, h],
            )
            for h in range(halves)
        ]
        for at in range(parts)
    ]
    for some in copies:
        for copy in some:
            copy.start()
    n, rows, stride = fine // 2, c.shape[1], side.shape[1] // c.shape[0]
    join = lambda pieces_of: jnp.concatenate(pieces_of, 1)
    tables = [unpack(table, place) for place in places]
    y_table = tables[-1]
    even, found = [], []
    for at in range(parts):
        for copy in copies[at]:
            copy.wait()
        whole = [
            join([u[k, h, at * size:(at + 1) * size, :] for h in range(halves)])
            for k in range(planes)
        ]
        even.append([
            join([u[k, h, pl.ds(at * size, size // 2, stride=2), :] for h in range(halves)])
            for k in range(0, planes, 2)
        ])
        found.append([
            [
                dot(tables[2 * at], cut(combine(z_a[z], whole), 0)),
                dot(tables[2 * at + 1], cut(combine(z_d[z], even[at]), 0)),
            ]
            for z in range(planes // 2)
        ])

    def whole_rows(values):
        own, out, tail = size // 2, [], None
        for at, value in enumerate(values):
            last = at == parts - 1
            before = 0 if at == 0 else 2 * reach
            inside = own - reach * ((at > 0) + (not last))
            if at:
                out.append(out.pop() + value[:before])
            out.append(value[before:before + inside])
            if not last:
                out.append(value[before + inside:before + inside + 2 * reach])
            if at == 0 or last:
                rest = value[value.shape[0] - (rows - n):]
                tail = rest if tail is None else tail + rest
        return jnp.concatenate(out + [tail], 0)

    for z in range(planes // 2):
        x_a = whole_rows([some[z][0] for some in found])
        x_d = whole_rows([some[z][1] for some in found])
        odd_lane = iota(x_d.shape, 1) % 2 == 1
        field = jnp.concatenate(
            [some[z] for some in even] + [jnp.zeros((rows - n, halves * lanes), F32)], 0
        )
        x_de = jnp.where(odd_lane, pltpu.roll(field, 1, 1), x_d)
        total = dot(join([cut(x_a, 1), cut(x_de, 1)]), y_table)
        total = total + jnp.where(odd_lane, 0.0, field)
        c[z] = total
        turned = total[:, :lanes].T
        index = iota((8, rows), 0)
        kept = jnp.where(index % 2 == 1, turned[:8], pltpu.roll(turned[8:16], 7, 0))
        side[:, z * stride:z * stride + rows] = kept
        if stride > rows:
            side[:, z * stride + rows:(z + 1) * stride] = jnp.zeros((8, stride - rows), F32)
    for k in range(planes):
        column[k:k + 1, :] = u[k, 0].T[:1, :]


def typed_rows(from_left, from_right, half):
    both = jnp.concatenate([from_left, from_right], 0)
    width = both.shape[1] // half
    rows = jnp.concatenate([both[:, z * width:(z + 1) * width] for z in range(half)], 0)
    kind = iota(rows.shape, 0) % 16
    even_lane = iota(rows.shape, 1) % 2 == 0
    field = jnp.where((kind >= 8) & (kind <= 10) & even_lane, rows, 0.0)
    a = jnp.where(kind < 4, rows, 0.0)
    d = jnp.where((kind >= 4) & (kind < 8) & even_lane, rows, 0.0)
    return jnp.concatenate([cut(a, 1), cut(d + pltpu.roll(field, 1, 1), 1)], 1), field


def join_kernel(half, side, column, left, right, y_sent, receive, message, again):
    from_left, from_right = left[...], right[...]
    typed, _ = typed_rows(from_left, from_right, half)
    sums = dot(y_sent[...], typed, ((1,), (1,)))[:8]
    part = iota(sums.shape, 1) // 32
    spread = jnp.concatenate([jnp.where(part == z, sums, 0.0) for z in range(half)], 0)
    added = dot(cut(spread, 1), receive[...])
    stride = side.shape[1] // half
    for z in range(half):
        here = slice(z * stride, (z + 1) * stride)
        message[:, here] = side[:, here] + added[8 * z:8 * z + 8]
    u0 = column[...]
    fine = u0.shape[1]
    width = from_right.shape[1] // half
    plane, lane = iota(u0.shape, 0), iota(u0.shape, 1)
    after = pltpu.roll(u0, fine - 1, 1)
    for z in range(half):
        for k, row in ((2 * z, 10), (2 * z + 1, 11)):
            corner = from_right[row:row + 1, z * width:z * width + 1]
            after = jnp.where((plane == k) & (lane == fine - 1), corner, after)
    before = pltpu.roll(u0, 1, 1)
    u0 = jnp.where(lane % 2 == 1, u0 - 0.5 * (before + after), u0)
    around = pltpu.roll(u0, 1, 0) + pltpu.roll(u0, 2 * half - 1, 0)
    message[:, half * stride:] = jnp.where(plane % 2 == 1, u0 - 0.5 * around, u0)
    again[...] = message[...]


def middle_kernel(
    z_a, z_d, places, c_own, block, left, right, table, out, w, edge, u, inner, ready, arrived, sent
):
    planes, halves, fine, lanes = u.shape[0], u.shape[1], block.shape[1], u.shape[3]
    cuts = (0, fine // 2 + 8, fine)
    copies = [
        [
            pltpu.make_async_copy(
                block.at[:, pl.ds(start, stop - start), pl.ds(h * lanes, lanes)],
                u.at[:, h, pl.ds(start, stop - start), :],
                arrived.at[turn, h],
            )
            for h in range(halves)
        ]
        for turn, (start, stop) in enumerate(zip(cuts, cuts[1:]))
    ]
    for some in copies:
        for copy in some:
            copy.start()
    half, rows, width = c_own.shape
    n, quarter = fine // 2, fine // 4
    from_left, from_right = left[...], right[...]
    typed, field = typed_rows(from_left, from_right, half)
    y_table, receive, x_level2, y_level2 = (unpack(table, place) for place in places)
    processed = dot(typed, y_table) + field
    lane = iota((rows, width), 1)
    row = iota((rows, width), 0)
    coarse, details = [], []
    for z in range(half):
        c = c_own[z] + dot(receive, cut(processed[32 * z:32 * z + 32], 0))
        coarse.append(c)
        around = pltpu.roll(c, 1, 0) + pltpu.roll(c, rows - 1, 0)
        c = jnp.where(row % 2 == 1, c - 0.5 * around, c)[:n]
        after = pltpu.roll(c, width - 2, 1)
        after = jnp.where(lane[:n] == width - 2, pltpu.roll(c, width - 1, 1), after)
        around = pltpu.roll(c, 2, 1) + after
        details.append(jnp.where(lane[:n] % 4 == 2, c - 0.5 * around, c))
    level = [dot(x_level2, cut(c, 0)) for c in coarse]
    level_a = [part[:quarter] for part in level]
    level_d = [part[quarter:] for part in level[::2]]
    for z in range(half):
        values = details[z]
        if z % 2:
            values = values - 0.5 * (details[z - 1] + details[(z + 1) % half])
        for h in range(halves):
            inner[z, h] = values[:, h * lanes:(h + 1) * lanes]
        if z % 2 == 0:
            a, d = combine(z_a[z // 2], level_a), combine(z_d[z // 2], level_d)
            added = dot(jnp.concatenate([cut(a, 1), cut(d, 1)], 1), y_level2)
            for h in range(halves):
                here = (z, h, pl.ds(0, quarter, stride=2), slice(None))
                inner[here] = inner[here] + added[:, h * lanes:(h + 1) * lanes]

    for k in range(planes):
        for h in range(halves):
            at = (k // 2) * width + h * lanes
            u[k, h, fine:fine + 1, :] = from_right[10 + k % 2:11 + k % 2, at:at + lanes]
    size = 32
    lane = iota((size, width), 1)
    odd_lane, last_lane = lane % 2 == 1, lane == width - 1

    def along_y(part):
        after = jnp.where(last_lane, 0.0, pltpu.roll(part, width - 1, 1))
        return jnp.where(odd_lane, part - 0.5 * (pltpu.roll(part, 1, 1) + after), part)

    def some_rows(step, carry):
        start, spot = step * 2 * size, step * size

        def rows_of(k):
            load = lambda first: jnp.concatenate(
                [u[k, h, pl.ds(first, size, stride=2), :] for h in range(halves)], 1
            )
            even = load(start)
            return even, load(start + 1) - 0.5 * (even + load(start + 2))

        def store(k, odd, part):
            for h in range(halves):
                target = w.at[k // 2, h] if k % 2 == 0 else (
                    edge.at[k // 2] if h == halves - 1 else ready.at[k // 2, h])
                target[pl.ds(start + odd, size, stride=2), :] = part[:, h * lanes:(h + 1) * lanes]

        begin = rows_of(0)
        here = begin
        for k in range(0, planes, 2):
            held = jnp.concatenate([inner[k // 2, h, pl.ds(spot, size), :] for h in range(halves)], 1)
            store(k, 0, jnp.where(odd_lane, along_y(here[0]), held))
            store(k, 1, along_y(here[1]))
            following = begin if k + 2 == planes else rows_of(k + 2)
            between = rows_of(k + 1)
            for odd in (0, 1):
                store(k + 1, odd, along_y(between[odd] - 0.5 * (here[odd] + following[odd])))
            here = following
        return carry

    done, steps = [], n // size
    for turn in range(2):
        for copy in copies[turn]:
            copy.wait()
        for step in range(turn * steps // 2, (turn + 1) * steps // 2):
            some_rows(step, 0)
        here = pl.ds(turn * n, n)
        for z in range(half):
            for h in range(halves - 1):
                done.append(pltpu.make_async_copy(
                    ready.at[z, h, here, :],
                    out.at[2 * z + 1, here, pl.ds(h * lanes, lanes)],
                    sent.at[turn, z, h],
                ))
                done[-1].start()
    for copy in done:
        copy.wait()


def last_kernel(
    z_a, z_d, left, right, x_level2, updates, w, edge, started, out, done, finished, sent
):
    half, halves, fine, lanes = w.shape
    n = fine // 2
    stride = (left.shape[1] - fine) // half
    from_left, from_right = left[...], right[...]
    column = from_right[:, half * stride:].T
    last = iota((fine, lanes), 1) == lanes - 1
    copies = []

    def send(source, k, h):
        copy = pltpu.make_async_copy(source, out.at[k, :, pl.ds(h * lanes, lanes)], sent.at[k, h])
        copy.start()
        copies.append(copy)

    def finish(values, k):
        return jnp.where(last, values - 0.5 * column[:, k:k + 1], values)

    for z in range(half):
        finished[z] = finish(edge[z], 2 * z + 1)
        send(finished.at[z], 2 * z + 1, halves - 1)
        for h in range(halves):
            done[z, h] = finish(w[z, h], 2 * z) if h == halves - 1 else w[z, h]
    both = jnp.concatenate([from_left, from_right], 0)
    sides = [both[:, z * stride:(z + 1) * stride] for z in range(half)]
    level = dot(cut(jnp.concatenate(sides, 0), 1), x_level2[...])
    lane = iota(sides[0].shape, 1)
    details = []
    for side in sides:
        around = pltpu.roll(side, 1, 1) + pltpu.roll(side, stride - 1, 1)
        details.append(jnp.where(lane % 2 == 1, side - 0.5 * around, side)[:, :n])
    quarter = n // 2
    level_a = [level[16 * z:16 * z + 16, :quarter] for z in range(half)]
    level_d = [level[16 * z:16 * z + 16, quarter:] for z in range(0, half, 2)]

    def update(factor, start):
        stop = start + factor.shape[0]
        table = jnp.concatenate([updates[piece, start:stop] for piece in range(3)], 0)
        return dot(cut(factor, 0), table, ((0,), (0,)))

    for z in range(half):
        if z % 2:
            factor = details[z] - 0.5 * (details[z - 1] + details[(z + 1) % half])
        else:
            factor = details[z]
            parts = [combine(z_a[z // 2], level_a), combine(z_d[z // 2], level_d)]
            coarse = update(jnp.concatenate(parts, 0), 16)
        added = update(factor, 0)
        for h in range(halves):
            here = (z, h, pl.ds(0, n, stride=2), slice(None))
            done[here] = done[here] + added[:, h * lanes:(h + 1) * lanes]
            if z % 2 == 0:
                here = (z, h, pl.ds(0, quarter, stride=4), slice(None))
                done[here] = done[here] + coarse[:, h * lanes:(h + 1) * lanes]
            send(done.at[z, h], 2 * z, h)
    for copy in copies:
        copy.wait()


def shards(density):
    planes, fine, width = density.shape
    half, n, lanes = planes // 2, fine // 2, 128
    halves = width // lanes
    depth = min(64, fine)
    z_a, z_d = z_tables(planes)
    z2_a, z2_d = z_tables(half)
    (own_a, own_d), send, x_receive, x2_a, x2_d = x_tables(fine)
    y_a, y_de, y2_a, y2_d, updates = y_tables(width)
    rows = n + 16
    stride = -(-rows // 128) * 128
    y_table = np.concatenate([pieces(y_a, 0), pieces(y_de, 0)], 0)
    sent = list(SENT.values())
    y_sent = np.zeros((16, y_table.shape[0]), y_table.dtype)
    y_sent[:len(sent)] = y_table[:, sent].T
    x_receive_t = np.zeros((32, stride))
    x_receive_t[:, :rows] = x_receive.T
    x2_t = np.zeros((stride, n))
    x2_t[:rows] = np.concatenate([x2_a.T, x2_d.T], 1)
    update = np.concatenate(updates, 0)
    high = update.astype(jnp.bfloat16)
    low = (update - high.astype(np.float64)).astype(jnp.bfloat16)
    params = lambda mib: pltpu.CompilerParams(vmem_limit_bytes=mib * 2**20)
    vmem = pl.BlockSpec(memory_space=pltpu.VMEM)
    hbm = pl.BlockSpec(memory_space=pltpu.HBM)
    shape = lambda *dims: jax.ShapeDtypeStruct(dims, F32)

    to_left, to_right = pl.pallas_call(
        functools.partial(edge_kernel, (send[0][:, :depth], send[1][:, fine - depth:]), z_a, z_d),
        out_shape=(shape(16, half * width),) * 2,
        in_specs=[hbm],
        out_specs=[vmem] * 2,
        scratch_shapes=[
            pltpu.VMEM((2, planes, halves, depth, lanes), F32),
            pltpu.SemaphoreType.DMA((2, halves)),
        ],
        compiler_params=params(50),
        name="edges",
    )(density)
    left_x, right_x = exchange(to_left, to_right, "gx")

    reach, parts = 16, 4
    size = n // parts
    own_tables = []
    for at in range(parts):
        near = list(range(max(0, at * size - reach), min(n, (at + 1) * size + reach)))
        if at in (0, parts - 1):
            near += list(range(n, rows))
        fine_at, even_at = slice(2 * at * size, 2 * (at + 1) * size), slice(at * size, (at + 1) * size)
        own_tables += [pieces(own_a[near][:, fine_at], 1), pieces(own_d[near][:, even_at], 1)]
    packed, places = pack(own_tables + [y_table], width)
    c_own, side, column = pl.pallas_call(
        functools.partial(own_kernel, z_a, z_d, reach, parts, places),
        out_shape=(shape(half, rows, width), shape(8, half * stride), shape(planes, fine)),
        in_specs=[hbm, vmem],
        out_specs=[vmem] * 3,
        scratch_shapes=[
            pltpu.VMEM((planes, halves, fine, lanes), F32),
            pltpu.SemaphoreType.DMA((parts, halves)),
        ],
        compiler_params=params(50),
        name="own",
    )(density, packed)

    to_left, to_right = pl.pallas_call(
        functools.partial(join_kernel, half),
        out_shape=(shape(8, half * stride + fine),) * 2,
        in_specs=[vmem] * 6,
        out_specs=[vmem] * 2,
        compiler_params=params(8),
        name="join",
    )(side, column, left_x, right_x, y_sent, pieces(np.tile(x_receive_t, (half, 1)), 0))
    left_y, right_y = exchange(to_left, to_right, "gy")

    x_level2 = pieces(np.concatenate([x2_a, x2_d], 0), 1)
    y_level2 = np.concatenate([pieces(y2_a, 0), pieces(y2_d, 0)], 0)
    packed, places = pack([y_table, pieces(x_receive, 1), x_level2, y_level2], width)
    started, w, edge = pl.pallas_call(
        functools.partial(middle_kernel, z2_a, z2_d, places),
        out_shape=(
            shape(planes, fine, width), shape(half, halves, fine, lanes), shape(half, fine, lanes),
        ),
        in_specs=[vmem, hbm, vmem, vmem, vmem],
        out_specs=[hbm, vmem, vmem],
        scratch_shapes=[
            pltpu.VMEM((planes, halves, fine + 8, lanes), F32),
            pltpu.VMEM((half, halves, n, lanes), F32),
            pltpu.VMEM((half, halves - 1, fine, lanes), F32),
            pltpu.SemaphoreType.DMA((2, halves)),
            pltpu.SemaphoreType.DMA((2, half, halves - 1)),
        ],
        compiler_params=params(44),
        name="middle",
    )(c_own, density, left_x, right_x, packed)

    return pl.pallas_call(
        functools.partial(last_kernel, z2_a, z2_d),
        out_shape=shape(planes, fine, width),
        in_specs=[vmem] * 6 + [hbm],
        out_specs=hbm,
        scratch_shapes=[
            pltpu.VMEM((half, halves, fine, lanes), F32),
            pltpu.VMEM((half, fine, lanes), F32),
            pltpu.SemaphoreType.DMA((planes, halves)),
        ],
        input_output_aliases={6: 0},
        compiler_params=params(16),
        name="last",
    )(left_y, right_y, pieces(x2_t, 0), np.stack([high, low, high]), w, edge, started)


def solution(mesh):
    spec = P(None, "gx", "gy")
    return jax.shard_map(shards, mesh=mesh, in_specs=(spec,), out_specs=spec, check_vma=False)
```
